128 devices in a mesh: blk: 8 (over y_lo, x), vslab: 16 (over z, y_hi, core).
Axes of the slice: x: 4, y: 4 (y_hi: 2, y_lo: 2; y = y_hi * 2 + y_lo), z: 4, core: 2. Of those that a mesh axis runs over, the one named last changes fastest.
Arguments:
- amplitudes: float32 [1024, 128, 800], P('blk', 'vslab'), may hold values from -6 to 6
- integrals: float32 [128, 800, 4096], P('vslab', None, 'blk'), may hold values from -0.01953125 to 0.01953125
- ab_energy: float32 [4096], P('blk'), may hold values from 1 to 4
- ij_energy: float32 [1024], replicated, may hold values from -4 to -1
- block_size: int32 [32], replicated, may hold values from 1 to 95, as said below
- block_owner: int32 [32], replicated, may hold values from 0 to 15, as said below
Outputs:
- amplitude_new: float32 [1024, 12288], P(None, ('blk', 'vslab'))
The draws below stay inside these ranges and needn't reach their ends.
Inputs may be any that keep to these rules, and one draw needn't show every extreme that they name: `block_size`: the blocks of one group fill its 512 pairs exactly; every owner holds at most 96 pairs, and one owner exactly 96. `block_owner`: every owner has two blocks.
All inputs are finite; a program needn't handle non-finite values.
Results may differ from the reference program's by a relative error of at most 0.00007.
Values sent between devices are 32-bit elements; how exact they have to be, the bound alone decides.
No kernel may reach another device: no remote copies, remote signals or barrier semaphores. Data moves between devices by JAX's collectives and lax.ppermute only.
A program may use at most 128 MiB of HBM per device.

```python
import jax
import jax.numpy as jnp
from jax import lax

NVIRT = 800
AB_B = 512
IJ_ALL = 1024
CVALS = 128
AB_ALL = 4096
OWNERS = 16
CAP = 96
N_BLK = 8
N_VSLAB = 16


def layout_tables(key):
    key_busy, key_weight, key_cut, key_order = jax.random.split(key, 4)
    owner_ids = jnp.arange(OWNERS, dtype=jnp.int32)
    busiest = jax.random.randint(key_busy, (), 0, OWNERS, dtype=jnp.int32)
    others = owner_ids != busiest
    weights = jnp.where(others, jax.random.randint(key_weight, (OWNERS,), 2, 5, dtype=jnp.int32), 0)
    remain = AB_B - CAP
    load = remain * weights // jnp.sum(weights)
    spare = remain - jnp.sum(load)
    first = jnp.where(busiest == 0, 1, 0)
    load = load + jnp.where(owner_ids == first, spare, 0)
    load = jnp.where(others, load, CAP).astype(jnp.int32)
    random_cut = 1 + jax.random.randint(key_cut, (OWNERS,), 0, load - 1, dtype=jnp.int32)
    cut_at = jnp.where(others, random_cut, 1).astype(jnp.int32)
    sizes = jnp.concatenate([cut_at, load - cut_at])
    tags = jnp.concatenate([owner_ids, owner_ids])
    order = jax.random.permutation(key_order, 2 * OWNERS)
    return (sizes[order].astype(jnp.int32), tags[order].astype(jnp.int32))


def draw_block_size(key, part):
    return layout_tables(key)[0]


def draw_block_owner(key, part):
    return layout_tables(key)[1]


def levels(own_key, dims, pieces, low, high):
    factor_of, own = 1.0, jax.random.fold_in(own_key, 6)
    for dim, blocks in pieces:
        draws = jnp.exp(jax.random.uniform(jax.random.fold_in(own, dim), (blocks,), jnp.float32, low / len(pieces), high / len(pieces)))
        factor_of = factor_of * jnp.repeat(draws, dims[dim] // blocks).reshape([-1 if axis == dim else 1 for axis in range(len(dims))])
    return factor_of


def noise(key, shape, scale, bound, shards=(), kind=jnp.bfloat16):
    result = jax.random.normal(key, shape, jnp.float32) * scale
    if len(shards) > 0:
        result = levels(key, shape, shards, -0.22, 0.18) * result
    return jnp.clip(result, min=-bound, max=bound).astype(kind)


def setup_inputs(seed: int = 0) -> dict:
    key_of = jax.random.split(jax.random.key(seed), 7)
    return {
        "amplitudes": noise(key_of[0], (IJ_ALL, CVALS, NVIRT), 1.0, 6.0, ((0, 8), (1, 16)), jnp.float32),
        "integrals": noise(key_of[1], (CVALS, NVIRT, AB_ALL), (CVALS * NVIRT) ** -0.5, 0.01953125, ((0, 16), (2, 8)), jnp.float32),
        "ab_energy": jnp.clip(1.0 + 3.0 * jax.random.uniform(key_of[2], (AB_ALL,), jnp.float32) ** levels(key_of[2], (AB_ALL,), ((0, 8),), -0.2, 0.2), 1.0, 4.0),
        "ij_energy": jnp.clip(jax.random.uniform(key_of[3], (IJ_ALL,), jnp.float32, -4.0, -1.0), -4.0, -1.0),
        "block_size": draw_block_size(jax.random.fold_in(key_of[6], 71), 0),
        "block_owner": draw_block_owner(jax.random.fold_in(key_of[6], 71), 0),
    }


def slot_tables(block_size, block_owner, rows, owners, cap):
    count = block_size.shape[0]
    order = jnp.arange(count, dtype=jnp.int32)
    starts = jnp.cumsum(block_size).astype(jnp.int32) - block_size
    same = block_owner[:, None] == block_owner[None, :]
    earlier = order[None, :] < order[:, None]
    before = jnp.sum(jnp.where(same & earlier, block_size[None, :], 0), axis=1).astype(jnp.int32)
    owner_hot = block_owner[:, None] == jnp.arange(owners, dtype=jnp.int32)[None, :]
    load = jnp.sum(jnp.where(owner_hot, block_size[:, None], 0), axis=0).astype(jnp.int32)
    owner_start = jnp.cumsum(load).astype(jnp.int32) - load
    block_base = jnp.sum(jnp.where(owner_hot, owner_start[None, :], 0), axis=1).astype(jnp.int32)
    shift_by = block_base + before - starts
    row_ids = jnp.arange(rows, dtype=jnp.int32)
    inside = (row_ids[:, None] >= starts[None, :]) & (row_ids[:, None] < (starts + block_size)[None, :])
    position = jnp.sum(jnp.where(inside, shift_by[None, :], 0), axis=1).astype(jnp.int32) + row_ids
    perm = jnp.zeros((rows,), jnp.int32).at[position].set(row_ids)
    slot_ids = jnp.arange(cap, dtype=jnp.int32)
    valid = slot_ids[None, :] < load[:, None]
    index = jnp.minimum(owner_start[:, None] + slot_ids[None, :], rows - 1)
    source = perm[index]
    return perm, owner_start, load, source, valid


def reference(amplitudes, integrals, ab_energy, ij_energy, block_size, block_owner):
    flat_t = amplitudes.reshape(amplitudes.shape[0], -1)
    flat_v = integrals.reshape(-1, integrals.shape[2])
    ladder = jnp.dot(flat_t, flat_v, precision=lax.Precision.HIGHEST, preferred_element_type=jnp.float32)
    perm, owner_start, load, source, valid = slot_tables(block_size, block_owner, AB_B, N_VSLAB, CAP)
    groups = jnp.arange(N_BLK, dtype=jnp.int32)[:, None] * AB_B
    columns = (groups + source.reshape(1, -1)).reshape(-1)
    picked = jnp.take(ladder, columns, axis=1)
    denom = jnp.take(ab_energy, columns)[None, :] - ij_energy[:, None]
    mask = jnp.tile(valid.reshape(-1), N_BLK)
    return jnp.where(mask[None, :], picked / denom, 0.0).astype(jnp.float32)
```

```python
import jax
import jax.numpy as jnp
from jax import lax
from jax.sharding import PartitionSpec as P


def slot_tables(block_size, block_owner, rows, owners, cap):
    count = block_size.shape[0]
    order = jnp.arange(count, dtype=jnp.int32)
    before_me = order[None, :] < order[:, None]
    starts = jnp.sum(jnp.where(before_me, block_size[None, :], 0), axis=1)
    same = block_owner[:, None] == block_owner[None, :]
    earlier = before_me
    before = jnp.sum(jnp.where(same & earlier, block_size[None, :], 0), axis=1)
    owner_hot = block_owner[:, None] == jnp.arange(owners, dtype=jnp.int32)[None, :]
    load = jnp.sum(jnp.where(owner_hot, block_size[:, None], 0), axis=0)
    owner_ids = jnp.arange(owners, dtype=jnp.int32)
    owner_start = jnp.sum(jnp.where(owner_ids[None, :] < owner_ids[:, None], load[None, :], 0), axis=1)
    block_base = jnp.sum(jnp.where(owner_hot, owner_start[None, :], 0), axis=1)
    shift_by = block_base + before - starts
    row_ids = jnp.arange(rows, dtype=jnp.int32)
    inside = (row_ids[:, None] >= starts[None, :]) & (
        row_ids[:, None] < (starts + block_size)[None, :]
    )
    position = jnp.sum(jnp.where(inside, shift_by[None, :], 0), axis=1) + row_ids
    perm = jnp.zeros((rows,), jnp.int32).at[position].set(row_ids)
    slot_ids = jnp.arange(cap, dtype=jnp.int32)
    valid = slot_ids[None, :] < load[:, None]
    index = jnp.minimum(owner_start[:, None] + slot_ids[None, :], rows - 1)
    source = perm[index]
    return (perm, owner_start, load, source, valid)


def on_device(amplitudes, integrals, ab_energy, ij_energy, block_size, block_owner):
    owners = lax.axis_size("vslab")
    rows = integrals.shape[2]
    cap = 3 * rows // owners
    v_matrix = integrals.reshape(-1, rows)
    t_tile = amplitudes.reshape(amplitudes.shape[0], -1)
    ladder = jnp.dot(
        lax.all_gather(t_tile, "blk", axis=0, tiled=True),
        v_matrix,
        precision=lax.Precision.HIGHEST,
        preferred_element_type=jnp.float32,
    )
    perm, owner_start, load, source, valid = slot_tables(block_size, block_owner, rows, owners, cap)
    mine = lax.axis_index("vslab")
    my_source = lax.dynamic_index_in_dim(source, mine, 0, keepdims=False)
    my_valid = lax.dynamic_index_in_dim(valid, mine, 0, keepdims=False)
    packed = jnp.take(ladder, source.reshape(-1), axis=1)
    packed = jnp.where(valid.reshape(1, -1), packed, 0.0).reshape(ladder.shape[0], owners, cap)
    received = lax.all_to_all(packed, "vslab", split_axis=1, concat_axis=1, tiled=True)
    summed = jnp.sum(received, axis=1)
    denom = jnp.take(ab_energy, my_source)[None, :] - ij_energy[:, None]
    return jnp.where(my_valid[None, :], summed / denom, 0.0)


def solution(mesh):
    placed = (P("blk", "vslab", None), P("vslab", None, "blk"), P("blk"), P(), P(), P())
    return jax.shard_map(
        on_device, mesh=mesh, in_specs=placed, out_specs=P(None, ("blk", "vslab")), check_vma=False
    )
```

```python
import jax
import jax.numpy as jnp
from jax import lax
from jax.sharding import PartitionSpec as P

NX, NY = 4, 2
STEPS = ((1, 0), (3, 0), (0, 1))
ROUNDS = (
    ((0, 1, (0, 0)), (1, 0, (0, 0)), (2, 0, (0, 0))),
    ((0, 0, (0, 0)), (1, 2, (0, 0)), (2, 1, (1, 0))),
    ((0, 2, (0, 0)), (1, 1, (1, 1)), (2, 2, (0, 0))),
    ((0, 2, (0, 1)), (1, 1, (0, 0)), (2, 0, (1, 0))),
    ((0, 1, (1, 0)), (1, 0, (3, 0)), (2, 1, (3, 0))),
    ((0, 2, (1, 0)), (1, 0, (0, 1)), (2, 2, (3, 0))),
    ((0, 0, (1, 1)), (1, 2, (3, 1)), (2, 1, (2, 0))),
)
BATCHES = (2, 3, 5)


def moved(offset, step):
    return ((offset[0] + step[0]) % NX, (offset[1] + step[1]) % NY)


def link_pairs(step):
    pairs = []
    for y in range(NY):
        for x in range(NX):
            to_x, to_y = moved((x, y), step)
            pairs.append((y * NX + x, to_y * NX + to_x))
    return pairs


def slot_of_pairs(block_size, block_owner, rows, cap):
    count = block_size.shape[0]
    order = jnp.arange(count, dtype=jnp.int32)
    earlier = order[None, :] < order[:, None]
    starts = jnp.sum(jnp.where(earlier, block_size[None, :], 0), axis=1)
    same = block_owner[:, None] == block_owner[None, :]
    before = jnp.sum(jnp.where(same & earlier, block_size[None, :], 0), axis=1)
    row_ids = jnp.arange(rows, dtype=jnp.int32)
    inside = (row_ids[:, None] >= starts[None, :]) & (
        row_ids[:, None] < (starts + block_size)[None, :]
    )
    base = block_owner * cap + before - starts
    return jnp.sum(jnp.where(inside, base[None, :], 0), axis=1) + row_ids


def on_device(amplitudes, integrals, ab_energy, ij_energy, block_size, block_owner):
    owners = lax.axis_size("vslab")
    ij_b = amplitudes.shape[0]
    rows = integrals.shape[2]
    cap = 3 * rows // owners
    v_matrix = integrals.reshape(-1, rows)
    t_own = amplitudes.transpose(1, 2, 0).reshape(-1, ij_b)
    depth = t_own.shape[0]
    cuts = [depth * i // 3 // 16 * 16 for i in range(3)] + [depth]
    v_piece = [v_matrix[cuts[i] : cuts[i + 1]] for i in range(3)]

    held = {(p, (0, 0)): t_own[cuts[p] : cuts[p + 1]] for p in range(3)}
    terms = {}

    dest = slot_of_pairs(block_size, block_owner, rows, cap)
    mine = lax.axis_index("vslab")
    slots = jnp.arange(cap, dtype=jnp.int32)
    relative = jnp.arange(owners, dtype=jnp.int32)
    near = (mine + relative // 2 % 4 * 4) % owners ^ (relative % 2 * 2) ^ (relative // 8)

    def one_hot(owner):
        at = (owner[:, None] * cap + slots[None, :]).reshape(-1)
        return (at[:, None] == dest[None, :]).astype(jnp.float32)

    half = owners // 2 * cap
    hot = one_hot(near)
    my_hot = hot[:cap]
    my_energy = jnp.sum(my_hot * ab_energy[None, :], axis=1)
    my_valid = jnp.sum(my_hot, axis=1) > 0.5

    def multiply(piece, offset):
        term = lax.dot_general(
            held[piece, offset],
            v_piece[piece],
            (((0,), (0,)), ((), ())),
            precision=lax.Precision.HIGH,
            preferred_element_type=jnp.float32,
        )
        terms[offset] = terms[offset] + term if offset in terms else term

    def pack(matrix, ladder):
        return lax.dot_general(
            matrix,
            ladder,
            (((1,), (1,)), ((), ())),
            precision=lax.Precision.HIGHEST,
            preferred_element_type=jnp.float32,
        )

    def sum_core(ladder):
        away = lax.ppermute(pack(hot[half:], ladder), "vslab", [(i, i ^ 1) for i in range(owners)])
        return pack(hot[:half], ladder) + away

    def sum_z(part):
        width = 2 * cap
        total = part[:width]
        for hop in range(1, 4):
            pairs = [(i, (i + 4 * hop) % owners) for i in range(owners)]
            total = total + lax.ppermute(part[hop * width : (hop + 1) * width], "vslab", pairs)
        return total

    def sum_y(part):
        return part[:cap] + lax.ppermute(part[cap:], "vslab", [(i, i ^ 2) for i in range(owners)])

    fresh = [(p, (0, 0)) for p in range(3)]
    count = {}
    at_core, at_z, parts, order = [], [], [], []
    for number, sends in enumerate(ROUNDS):
        arrived = {}
        for link, p, offset in sends:
            to = moved(offset, STEPS[link])
            arrived[p, to] = lax.ppermute(held[p, offset], "blk", link_pairs(STEPS[link]))
        parts += [sum_y(part) for part in at_z]
        at_z = [sum_z(part) for part in at_core]
        at_core = []
        for p, offset in fresh:
            multiply(p, offset)
            count[offset] = count.get(offset, 0) + 1
        if number - 1 in BATCHES:
            batch = [o for o in terms if count[o] == 3]
            at_core.append(sum_core(jnp.concatenate([terms.pop(o) for o in batch], axis=0)))
            order += batch
            if number + 1 == len(ROUNDS):
                at_z.append(sum_z(at_core.pop()))
        fresh = list(arrived)
        held.update(arrived)
        h_keys, t_keys = list(held), list(terms)
        h, t, at_core, at_z, parts = lax.optimization_barrier(
            ([held[k] for k in h_keys], [terms[k] for k in t_keys], at_core, at_z, parts)
        )
        held, terms = dict(zip(h_keys, h)), dict(zip(t_keys, t))
    for p, offset in fresh:
        multiply(p, offset)
    ((last, ladder),) = terms.items()
    order.append(last)
    at_z.append(sum_z(sum_core(ladder)))
    parts.append(sum_y(jnp.concatenate(at_z, axis=1)))

    me = lax.axis_index("blk")
    my_x, my_y = me % NX, me // NX
    everything = jnp.concatenate(parts, axis=1)
    place = [NX * dy + dx for dx, dy in order]
    place_of = jnp.array([place.index(k) for k in range(NX * NY)], jnp.int32)
    columns = []
    for source in range(NX * NY):
        dx = (my_x + NX - source % NX) % NX
        dy = (my_y + NY - source // NX) % NY
        start = place_of[dy * NX + dx] * ij_b
        columns.append(lax.dynamic_slice_in_dim(everything, start, ij_b, axis=1))
    full = jnp.concatenate(columns, axis=1)
    denom = my_energy[:, None] - ij_energy[None, :]
    return jnp.where(my_valid[:, None], full / denom, 0.0).T


def solution(mesh):
    placed = (P("blk", "vslab", None), P("vslab", None, "blk"), P("blk"), P(), P(), P())
    return jax.shard_map(
        on_device, mesh=mesh, in_specs=placed, out_specs=P(None, ("blk", "vslab")), check_vma=False
    )
```

```python
import jax
import jax.numpy as jnp
from jax import lax
from jax.experimental import pallas as pl
from jax.experimental.pallas import tpu as pltpu
from jax.sharding import PartitionSpec as P

NX, NY = 4, 2
STEPS = ((1, 0), (3, 0), (0, 1))
ROUNDS = (
    ((0, 1, (0, 0)), (1, 0, (0, 0)), (2, 0, (0, 0))),
    ((0, 0, (0, 0)), (1, 2, (0, 0)), (2, 1, (1, 0))),
    ((0, 2, (0, 0)), (1, 1, (1, 1)), (2, 2, (0, 0))),
    ((0, 2, (0, 1)), (1, 1, (0, 0)), (2, 0, (1, 0))),
    ((0, 1, (1, 0)), (1, 0, (3, 0)), (2, 1, (3, 0))),
    ((0, 2, (1, 0)), (1, 0, (0, 1)), (2, 2, (3, 0))),
    ((0, 0, (1, 1)), (1, 2, (3, 1)), (2, 1, (2, 0))),
)
BATCHES = (
    {"blocks": 1, "pack": 0, "core": 1, "near": 2, "far": 3},
    {"blocks": 2, "pack": 3, "core": 4, "near": 5, "far": 6},
    {"blocks": 2, "pack": 4, "core": 5, "near": 6},
    {"blocks": 2, "pack": 6},
    {"blocks": 1},
)
NEXT = ("pack", "core", "near", "far", "y")


def moved(offset, step):
    return ((offset[0] + step[0]) % NX, (offset[1] + step[1]) % NY)


def link_pairs(step):
    pairs = []
    for y in range(NY):
        for x in range(NX):
            to_x, to_y = moved((x, y), step)
            pairs.append((y * NX + x, to_y * NX + to_x))
    return pairs


def slot_of_pairs(block_size, block_owner, rows, cap):
    count = block_size.shape[0]
    order = jnp.arange(count, dtype=jnp.int32)
    earlier = order[None, :] < order[:, None]
    starts = jnp.sum(jnp.where(earlier, block_size[None, :], 0), axis=1)
    same = block_owner[:, None] == block_owner[None, :]
    before = jnp.sum(jnp.where(same & earlier, block_size[None, :], 0), axis=1)
    row_ids = jnp.arange(rows, dtype=jnp.int32)
    inside = (row_ids[:, None] >= starts[None, :]) & (
        row_ids[:, None] < (starts + block_size)[None, :]
    )
    base = block_owner * cap + before - starts
    return jnp.sum(jnp.where(inside, base[None, :], 0), axis=1) + row_ids


CHEAP = pl.CostEstimate(flops=1, bytes_accessed=1, transcendentals=0)
PARAMS = pltpu.CompilerParams(vmem_limit_bytes=14 * 2**20)
F32 = jnp.float32


def halves(x):
    high = x.astype(jnp.bfloat16)
    return high, (x - high.astype(F32)).astype(jnp.bfloat16)


def product_kernel(t_ref, v_ref, out_ref):
    t_high, t_low = halves(t_ref[...])
    v_high, v_low = halves(v_ref[...])

    def dot(t, v):
        return lax.dot_general(t, v, (((0,), (0,)), ((), ())), preferred_element_type=F32)

    term = dot(t_high, v_high) + (dot(t_high, v_low) + dot(t_low, v_high))

    @pl.when(pl.program_id(0) == 0)
    def _():
        out_ref[...] = term

    @pl.when(pl.program_id(0) > 0)
    def _():
        out_ref[...] += term


def product(t, v, first):
    depth, rows = t.shape
    steps = 4 if depth % 64 == 0 else 2
    tile, width = depth // steps, v.shape[1]
    return pl.pallas_call(
        product_kernel,
        grid=(steps,),
        in_specs=[
            pl.BlockSpec((tile, rows), lambda k: (k, 0)),
            pl.BlockSpec((pl.Element(tile), pl.Element(width)), lambda k: (pl.multiple_of(first + k * tile, 16), 0)),
        ],
        out_specs=pl.BlockSpec((rows, width), lambda k: (0, 0)),
        out_shape=jax.ShapeDtypeStruct((rows, width), F32),
        cost_estimate=CHEAP,
        compiler_params=PARAMS,
        name="product",
    )(t, v)


def pack_kernel(hot_ref, p_ref, out_ref):
    rest, total = p_ref[...], None
    for _ in range(3):
        part = rest.astype(jnp.bfloat16)
        rest = rest - part.astype(F32)
        term = lax.dot_general(hot_ref[...], part, (((1,), (1,)), ((), ())), preferred_element_type=F32)
        total = term if total is None else total + term
    out_ref[...] = total


def pack(hot, ladder):
    tile = hot.shape[0] // 4
    return pl.pallas_call(
        pack_kernel,
        grid=(4,),
        in_specs=[
            pl.BlockSpec((tile, hot.shape[1]), lambda k: (k, 0)),
            pl.BlockSpec(ladder.shape, lambda k: (0, 0)),
        ],
        out_specs=pl.BlockSpec((tile, ladder.shape[0]), lambda k: (k, 0)),
        out_shape=jax.ShapeDtypeStruct((hot.shape[0], ladder.shape[0]), F32),
        cost_estimate=CHEAP,
        compiler_params=PARAMS,
        name="pack",
    )(hot, ladder)


def on_device(amplitudes, integrals, ab_energy, ij_energy, block_size, block_owner):
    owners = lax.axis_size("vslab")
    ij_b = amplitudes.shape[0]
    rows = integrals.shape[2]
    cap = 3 * rows // owners
    v_matrix = integrals.reshape(-1, rows)
    t_own = amplitudes.transpose(1, 2, 0).reshape(-1, ij_b)
    depth = t_own.shape[0]
    cuts = [0, depth // 96 // 2 * 64, depth - depth // 96 * 32 - 32, depth]

    held = {(p, (0, 0)): t_own[cuts[p] : cuts[p + 1]] for p in range(3)}
    terms = {}

    dest = slot_of_pairs(block_size, block_owner, rows, cap)
    mine = lax.axis_index("vslab")
    slots = jnp.arange(cap, dtype=jnp.int32)
    apart = jnp.array([c + 4 * z + 2 * y for c in (0, 1) for z in (0, 2, 1, 3) for y in (0, 1)], jnp.int32)
    near = mine ^ apart

    def one_hot(owner):
        at = (owner[:, None] * cap + slots[None, :]).reshape(-1)
        return (at[:, None] == dest[None, :]).astype(jnp.bfloat16)

    hot = one_hot(near)
    my_hot = hot[:cap] > 0.5
    my_energy = jnp.sum(jnp.where(my_hot, ab_energy[None, :], 0.0), axis=1)
    my_valid = jnp.any(my_hot, axis=1)

    def multiply(piece, offset):
        term = product(held[piece, offset], v_matrix, cuts[piece])
        terms[offset] = terms[offset] + term if offset in terms else term

    def swap(part, bits):
        return lax.ppermute(part, "vslab", [(i, i ^ bits) for i in range(owners)])

    def fold(part, bits):
        middle = part.shape[0] // 2
        return part[:middle] + swap(part[middle:], bits)

    def sum_z(part):
        width = 2 * cap
        total = part[:width]
        for k, bits in enumerate((8, 4, 12)):
            total = total + swap(part[(k + 1) * width : (k + 2) * width], bits)
        return total

    def step(name, part):
        if name == "pack":
            return pack(hot, part)
        return fold(part, {"core": 1, "near": 4, "far": 8, "y": 2}[name])

    fresh = [(p, (0, 0)) for p in range(3)]
    count = {}
    parts, order = [], []

    def start_batches():
        while len(parts) < len(BATCHES):
            batch = [o for o in terms if count[o] == 3][: BATCHES[len(parts)]["blocks"]]
            if len(batch) < BATCHES[len(parts)]["blocks"]:
                break
            parts.append(jnp.concatenate([terms.pop(o) for o in batch], axis=0))
            order.extend(batch)

    for number, sends in enumerate(ROUNDS):
        arrived = {}
        for link, p, offset in sends:
            to = moved(offset, STEPS[link])
            arrived[p, to] = lax.ppermute(held[p, offset], "blk", link_pairs(STEPS[link]))
        for p, offset in fresh:
            multiply(p, offset)
            count[offset] = count.get(offset, 0) + 1
        start_batches()
        for i, batch in enumerate(BATCHES[: len(parts)]):
            for name in NEXT:
                if batch.get(name) == number:
                    parts[i] = step(name, parts[i])
        fresh = list(arrived)
        held.update(arrived)
        h_keys, t_keys = list(held), list(terms)
        h, t, parts = lax.optimization_barrier(([held[k] for k in h_keys], [terms[k] for k in t_keys], parts))
        held, terms = dict(zip(h_keys, h)), dict(zip(t_keys, t))
    for p, offset in fresh:
        multiply(p, offset)
        count[offset] = count.get(offset, 0) + 1
    start_batches()
    own, first, second, third, last = parts
    last = jnp.concatenate([third, step("pack", last)], axis=1)
    last, second, own, first = lax.optimization_barrier((last, second, own, first))
    last = step("core", last)
    second = step("far", second)
    last, second, own, first = lax.optimization_barrier((last, second, own, first))
    last = sum_z(last)
    settled = step("y", jnp.concatenate([own, first], axis=1))
    last, second, settled = lax.optimization_barrier((last, second, settled))
    parts = [settled, step("y", jnp.concatenate([second, last], axis=1))]

    me = lax.axis_index("blk")
    my_x, my_y = me % NX, me // NX
    everything = jnp.concatenate(parts, axis=1)
    place = [NX * dy + dx for dx, dy in order]
    place_of = jnp.array([place.index(k) for k in range(NX * NY)], jnp.int32)
    columns = []
    for source in range(NX * NY):
        dx = (my_x + NX - source % NX) % NX
        dy = (my_y + NY - source // NX) % NY
        start = place_of[dy * NX + dx] * ij_b
        columns.append(lax.dynamic_slice_in_dim(everything, start, ij_b, axis=1))
    full = jnp.concatenate(columns, axis=1)
    denom = my_energy[:, None] - ij_energy[None, :]
    return jnp.where(my_valid[:, None], full / denom, 0.0).T


def solution(mesh):
    placed = (P("blk", "vslab", None), P("vslab", None, "blk"), P("blk"), P(), P(), P())
    return jax.shard_map(
        on_device, mesh=mesh, in_specs=placed, out_specs=P(None, ("blk", "vslab")), check_vma=False
    )
```

```python
import jax
import jax.numpy as jnp
from jax import lax
from jax.experimental import pallas as pl
from jax.experimental.pallas import tpu as pltpu
from jax.sharding import PartitionSpec as P

NX, NY = 4, 2
STEPS = ((1, 0), (3, 0), (0, 1))
ROUNDS = (
    ((0, 1, (0, 0)), (1, 0, (0, 0)), (2, 0, (0, 0))),
    ((0, 0, (0, 0)), (1, 2, (0, 0)), (2, 1, (1, 0))),
    ((0, 2, (0, 0)), (1, 1, (1, 1)), (2, 2, (0, 0))),
    ((0, 2, (0, 1)), (1, 1, (0, 0)), (2, 0, (1, 0))),
    ((0, 1, (1, 0)), (1, 0, (3, 0)), (2, 1, (3, 0))),
    ((0, 2, (1, 0)), (1, 0, (0, 1)), (2, 2, (3, 0))),
    ((0, 0, (1, 1)), (1, 2, (3, 1)), (2, 1, (2, 0))),
)
BATCHES = (
    {"blocks": 1, "pack": 0, "core": 1, "near": 2, "far": 3},
    {"blocks": 2, "pack": 3, "core": 4, "near": 5, "far": 6},
    {"blocks": 2, "pack": 4, "core": 5, "near": 6},
    {"blocks": 2, "pack": 6},
    {"blocks": 1},
)
NEXT = ("pack", "core", "near", "far", "y")


def moved(offset, step):
    return ((offset[0] + step[0]) % NX, (offset[1] + step[1]) % NY)


def link_pairs(step):
    pairs = []
    for y in range(NY):
        for x in range(NX):
            to_x, to_y = moved((x, y), step)
            pairs.append((y * NX + x, to_y * NX + to_x))
    return pairs


def slot_of_pairs(block_size, block_owner, rows, cap):
    count = block_size.shape[0]
    order = jnp.arange(count, dtype=jnp.int32)
    earlier = order[None, :] < order[:, None]
    starts = jnp.sum(jnp.where(earlier, block_size[None, :], 0), axis=1)
    same = block_owner[:, None] == block_owner[None, :]
    before = jnp.sum(jnp.where(same & earlier, block_size[None, :], 0), axis=1)
    row_ids = jnp.arange(rows, dtype=jnp.int32)
    inside = (row_ids[:, None] >= starts[None, :]) & (
        row_ids[:, None] < (starts + block_size)[None, :]
    )
    base = block_owner * cap + before - starts
    return jnp.sum(jnp.where(inside, base[None, :], 0), axis=1) + row_ids


CHEAP = pl.CostEstimate(flops=1, bytes_accessed=1, transcendentals=0)
PARAMS = pltpu.CompilerParams(vmem_limit_bytes=14 * 2**20)
F32 = jnp.float32


def halves(x):
    high = x.astype(jnp.bfloat16)
    return high, (x - high.astype(F32)).astype(jnp.bfloat16)


def product_kernel(t_ref, v_ref, out_ref):
    t_high, t_low = halves(t_ref[...])
    v_high, v_low = halves(v_ref[...])

    def dot(t, v):
        return lax.dot_general(t, v, (((0,), (0,)), ((), ())), preferred_element_type=F32)

    term = dot(t_high, v_high) + (dot(t_high, v_low) + dot(t_low, v_high))

    @pl.when(pl.program_id(0) == 0)
    def _():
        out_ref[...] = term

    @pl.when(pl.program_id(0) > 0)
    def _():
        out_ref[...] += term


def product(t, v, first):
    depth, rows = t.shape
    steps = 4 if depth % 64 == 0 else 2
    tile, width = depth // steps, v.shape[1]
    return pl.pallas_call(
        product_kernel,
        grid=(steps,),
        in_specs=[
            pl.BlockSpec((tile, rows), lambda k: (k, 0)),
            pl.BlockSpec((pl.Element(tile), pl.Element(width)), lambda k: (pl.multiple_of(first + k * tile, 16), 0)),
        ],
        out_specs=pl.BlockSpec((rows, width), lambda k: (0, 0)),
        out_shape=jax.ShapeDtypeStruct((rows, width), F32),
        cost_estimate=CHEAP,
        compiler_params=PARAMS,
        name="product",
    )(t, v)


def pack_kernel(hot_ref, p_ref, out_ref):
    rest, total = p_ref[...], None
    for _ in range(3):
        part = rest.astype(jnp.bfloat16)
        rest = rest - part.astype(F32)
        term = lax.dot_general(hot_ref[...], part, (((1,), (1,)), ((), ())), preferred_element_type=F32)
        total = term if total is None else total + term
    out_ref[...] = total


def pack(hot, ladder):
    tile = hot.shape[0] // 4
    return pl.pallas_call(
        pack_kernel,
        grid=(4,),
        in_specs=[
            pl.BlockSpec((tile, hot.shape[1]), lambda k: (k, 0)),
            pl.BlockSpec(ladder.shape, lambda k: (0, 0)),
        ],
        out_specs=pl.BlockSpec((tile, ladder.shape[0]), lambda k: (k, 0)),
        out_shape=jax.ShapeDtypeStruct((hot.shape[0], ladder.shape[0]), F32),
        cost_estimate=CHEAP,
        compiler_params=PARAMS,
        name="pack",
    )(hot, ladder)


def on_device(amplitudes, integrals, ab_energy, ij_energy, block_size, block_owner):
    owners = lax.axis_size("vslab")
    ij_b = amplitudes.shape[0]
    rows = integrals.shape[2]
    cap = 3 * rows // owners
    v_matrix = integrals.reshape(-1, rows)
    t_own = amplitudes.transpose(1, 2, 0).reshape(-1, ij_b)
    depth = t_own.shape[0]
    cuts = [0, depth // 96 // 2 * 64, depth - depth // 96 * 32 - 32, depth]

    held = {(p, (0, 0)): t_own[cuts[p] : cuts[p + 1]] for p in range(3)}
    terms = {}

    dest = slot_of_pairs(block_size, block_owner, rows, cap)
    mine = lax.axis_index("vslab")
    slots = jnp.arange(cap, dtype=jnp.int32)
    apart = jnp.array([c + 4 * z + 2 * y for c in (0, 1) for z in (0, 2, 1, 3) for y in (0, 1)], jnp.int32)
    near = mine ^ apart

    def one_hot(owner):
        at = (owner[:, None] * cap + slots[None, :]).reshape(-1)
        return (at[:, None] == dest[None, :]).astype(jnp.bfloat16)

    hot = one_hot(near)
    my_hot = hot[:cap] > 0.5
    my_energy = jnp.sum(jnp.where(my_hot, ab_energy[None, :], 0.0), axis=1)
    my_valid = jnp.any(my_hot, axis=1)

    def multiply(piece, offset):
        term = product(held[piece, offset], v_matrix, cuts[piece])
        terms[offset] = terms[offset] + term if offset in terms else term

    def swap(part, bits):
        return lax.ppermute(part, "vslab", [(i, i ^ bits) for i in range(owners)])

    def fold(part, bits):
        middle = part.shape[0] // 2
        return part[:middle] + swap(part[middle:], bits)

    def sum_z(part):
        width = 2 * cap
        total = part[:width]
        for k, bits in enumerate((8, 4, 12)):
            total = total + swap(part[(k + 1) * width : (k + 2) * width], bits)
        return total

    def step(name, part):
        if name == "pack":
            return pack(hot, part)
        return fold(part, {"core": 1, "near": 4, "far": 8, "y": 2}[name])

    fresh = [(p, (0, 0)) for p in range(3)]
    count = {}
    parts, order = [], []

    def start_batches():
        while len(parts) < len(BATCHES):
            batch = [o for o in terms if count[o] == 3][: BATCHES[len(parts)]["blocks"]]
            if len(batch) < BATCHES[len(parts)]["blocks"]:
                break
            parts.append(jnp.concatenate([terms.pop(o) for o in batch], axis=0))
            order.extend(batch)

    for number, sends in enumerate(ROUNDS):
        arrived = {}
        for link, p, offset in sends:
            to = moved(offset, STEPS[link])
            arrived[p, to] = lax.ppermute(held[p, offset], "blk", link_pairs(STEPS[link]))
        for p, offset in fresh:
            multiply(p, offset)
            count[offset] = count.get(offset, 0) + 1
        start_batches()
        for i, batch in enumerate(BATCHES[: len(parts)]):
            for name in NEXT:
                if batch.get(name) == number:
                    parts[i] = step(name, parts[i])
        fresh = list(arrived)
        held.update(arrived)
        h_keys, t_keys = list(held), list(terms)
        h, t, parts = lax.optimization_barrier(([held[k] for k in h_keys], [terms[k] for k in t_keys], parts))
        held, terms = dict(zip(h_keys, h)), dict(zip(t_keys, t))
    for p, offset in fresh:
        multiply(p, offset)
        count[offset] = count.get(offset, 0) + 1
    start_batches()
    early, (second, third, last) = jnp.concatenate(parts[:2], axis=1), parts[2:]
    last = step("pack", last)
    third = step("core", third)
    last, third, second, early = lax.optimization_barrier((last, third, second, early))
    last = step("core", last)
    third = sum_z(third)
    last, third, second, early = lax.optimization_barrier((last, third, second, early))
    last = sum_z(last)
    second = step("far", second)
    early = step("y", jnp.concatenate([early, third], axis=1))
    last, second, early = lax.optimization_barrier((last, second, early))
    parts = [early, step("y", jnp.concatenate([second, last], axis=1))]
    order = order[:3] + order[5:7] + order[3:5] + order[7:]

    me = lax.axis_index("blk")
    my_x, my_y = me % NX, me // NX
    everything = jnp.concatenate(parts, axis=1)
    place = [NX * dy + dx for dx, dy in order]
    place_of = jnp.array([place.index(k) for k in range(NX * NY)], jnp.int32)
    columns = []
    for source in range(NX * NY):
        dx = (my_x + NX - source % NX) % NX
        dy = (my_y + NY - source // NX) % NY
        start = place_of[dy * NX + dx] * ij_b
        columns.append(lax.dynamic_slice_in_dim(everything, start, ij_b, axis=1))
    full = jnp.concatenate(columns, axis=1)
    denom = my_energy[:, None] - ij_energy[None, :]
    return jnp.where(my_valid[:, None], full / denom, 0.0).T


def solution(mesh):
    placed = (P("blk", "vslab", None), P("vslab", None, "blk"), P("blk"), P(), P(), P())
    return jax.shard_map(
        on_device, mesh=mesh, in_specs=placed, out_specs=P(None, ("blk", "vslab")), check_vma=False
    )
```

```python
import jax
import jax.numpy as jnp
from jax import lax
from jax.experimental import pallas as pl
from jax.experimental.pallas import tpu as pltpu
from jax.sharding import PartitionSpec as P

NX, NY = 4, 2
STEPS = ((1, 0), (3, 0), (0, 1))
ROUNDS = (
    ((0, 0, (0, 0)), (1, 0, (0, 0)), (2, 0, (0, 0))),
    ((0, 2, (0, 0)), (1, 1, (0, 0)), (2, 2, (0, 0))),
    ((0, 1, (0, 0)), (1, 2, (0, 0)), (2, 1, (3, 0))),
    ((0, 1, (3, 1)), (1, 2, (0, 1)), (2, 0, (3, 0))),
    ((0, 0, (0, 1)), (1, 2, (3, 0)), (2, 1, (1, 0))),
    ((0, 0, (1, 0)), (1, 1, (3, 0)), (2, 2, (1, 0))),
    ((0, 1, (1, 1)), (1, 0, (3, 1)), (2, 2, (2, 0))),
)
BATCHES = (
    {"blocks": 1, "pack": 0, "core": 1, "near": 2, "far": 3},
    {"blocks": 2, "pack": 3, "core": 4, "near": 5, "far": 6},
    {"blocks": 2, "pack": 4, "core": 5, "near": 6},
    {"blocks": 2, "pack": 6},
    {"blocks": 1},
)
NEXT = ("pack", "core", "near", "far", "y")


def moved(offset, step):
    return ((offset[0] + step[0]) % NX, (offset[1] + step[1]) % NY)


def link_pairs(step):
    pairs = []
    for y in range(NY):
        for x in range(NX):
            to_x, to_y = moved((x, y), step)
            pairs.append((y * NX + x, to_y * NX + to_x))
    return pairs


def slot_of_pairs(block_size, block_owner, rows, cap):
    count = block_size.shape[0]
    order = jnp.arange(count, dtype=jnp.int32)
    earlier = order[None, :] < order[:, None]
    starts = jnp.sum(jnp.where(earlier, block_size[None, :], 0), axis=1)
    same = block_owner[:, None] == block_owner[None, :]
    before = jnp.sum(jnp.where(same & earlier, block_size[None, :], 0), axis=1)
    row_ids = jnp.arange(rows, dtype=jnp.int32)
    inside = (row_ids[:, None] >= starts[None, :]) & (
        row_ids[:, None] < (starts + block_size)[None, :]
    )
    base = block_owner * cap + before - starts
    return jnp.sum(jnp.where(inside, base[None, :], 0), axis=1) + row_ids


CHEAP = pl.CostEstimate(flops=1, bytes_accessed=1, transcendentals=0)
PARAMS = pltpu.CompilerParams(vmem_limit_bytes=14 * 2**20)
F32 = jnp.float32


def halves(x):
    high = x.astype(jnp.bfloat16)
    return high, (x - high.astype(F32)).astype(jnp.bfloat16)


def product_kernel(t_ref, v_ref, out_ref):
    t_high, t_low = halves(t_ref[...])
    v_high, v_low = halves(v_ref[...])

    def dot(t, v):
        return lax.dot_general(t, v, (((0,), (0,)), ((), ())), preferred_element_type=F32)

    term = dot(t_high, v_high) + (dot(t_high, v_low) + dot(t_low, v_high))

    @pl.when(pl.program_id(0) == 0)
    def _():
        out_ref[...] = term

    @pl.when(pl.program_id(0) > 0)
    def _():
        out_ref[...] += term


def product(t, v, first):
    depth, rows = t.shape
    steps = 4 if depth % 64 == 0 else 2
    tile, width = depth // steps, v.shape[1]
    return pl.pallas_call(
        product_kernel,
        grid=(steps,),
        in_specs=[
            pl.BlockSpec((tile, rows), lambda k: (k, 0)),
            pl.BlockSpec((pl.Element(tile), pl.Element(width)), lambda k: (pl.multiple_of(first + k * tile, 16), 0)),
        ],
        out_specs=pl.BlockSpec((rows, width), lambda k: (0, 0)),
        out_shape=jax.ShapeDtypeStruct((rows, width), F32),
        cost_estimate=CHEAP,
        compiler_params=PARAMS,
        name="product",
    )(t, v)


def pack_kernel(hot_ref, p_ref, out_ref):
    rest, total = p_ref[...], None
    for _ in range(3):
        part = rest.astype(jnp.bfloat16)
        rest = rest - part.astype(F32)
        term = lax.dot_general(hot_ref[...], part, (((1,), (1,)), ((), ())), preferred_element_type=F32)
        total = term if total is None else total + term
    out_ref[...] = total


def pack(hot, ladder):
    tile = hot.shape[0] // 4
    return pl.pallas_call(
        pack_kernel,
        grid=(4,),
        in_specs=[
            pl.BlockSpec((tile, hot.shape[1]), lambda k: (k, 0)),
            pl.BlockSpec(ladder.shape, lambda k: (0, 0)),
        ],
        out_specs=pl.BlockSpec((tile, ladder.shape[0]), lambda k: (k, 0)),
        out_shape=jax.ShapeDtypeStruct((hot.shape[0], ladder.shape[0]), F32),
        cost_estimate=CHEAP,
        compiler_params=PARAMS,
        name="pack",
    )(hot, ladder)


def on_device(amplitudes, integrals, ab_energy, ij_energy, block_size, block_owner):
    owners = lax.axis_size("vslab")
    ij_b = amplitudes.shape[0]
    rows = integrals.shape[2]
    cap = 3 * rows // owners
    v_matrix = integrals.reshape(-1, rows)
    t_own = amplitudes.transpose(1, 2, 0).reshape(-1, ij_b)
    depth = t_own.shape[0]
    cuts = [0, depth // 96 // 2 * 64, depth - depth // 96 * 32 - 32, depth]

    held = {(p, (0, 0)): t_own[cuts[p] : cuts[p + 1]] for p in range(3)}
    terms = {}

    dest = slot_of_pairs(block_size, block_owner, rows, cap)
    mine = lax.axis_index("vslab")
    slots = jnp.arange(cap, dtype=jnp.int32)
    apart = jnp.array([c + 4 * z + 2 * y for c in (0, 1) for z in (0, 2, 1, 3) for y in (0, 1)], jnp.int32)
    near = mine ^ apart

    def one_hot(owner):
        at = (owner[:, None] * cap + slots[None, :]).reshape(-1)
        return (at[:, None] == dest[None, :]).astype(jnp.bfloat16)

    hot = one_hot(near)
    my_hot = hot[:cap] > 0.5
    my_energy = jnp.sum(jnp.where(my_hot, ab_energy[None, :], 0.0), axis=1)
    my_valid = jnp.any(my_hot, axis=1)

    def multiply(piece, offset):
        term = product(held[piece, offset], v_matrix, cuts[piece])
        terms[offset] = terms[offset] + term if offset in terms else term

    def swap(part, bits):
        return lax.ppermute(part, "vslab", [(i, i ^ bits) for i in range(owners)])

    def fold(part, bits):
        middle = part.shape[0] // 2
        return part[:middle] + swap(part[middle:], bits)

    def sum_z(part):
        width = 2 * cap
        total = part[:width]
        for k, bits in enumerate((8, 4, 12)):
            total = total + swap(part[(k + 1) * width : (k + 2) * width], bits)
        return total

    def step(name, part):
        if name == "pack":
            return pack(hot, part)
        return fold(part, {"core": 1, "near": 4, "far": 8, "y": 2}[name])

    fresh = [(p, (0, 0)) for p in range(3)]
    count = {}
    parts, order = [], []

    def start_batches():
        while len(parts) < len(BATCHES):
            batch = [o for o in terms if count[o] == 3][: BATCHES[len(parts)]["blocks"]]
            if len(batch) < BATCHES[len(parts)]["blocks"]:
                break
            parts.append(jnp.concatenate([terms.pop(o) for o in batch], axis=0))
            order.extend(batch)

    for number, sends in enumerate(ROUNDS):
        arrived = {}
        for link, p, offset in sends:
            to = moved(offset, STEPS[link])
            arrived[p, to] = lax.ppermute(held[p, offset], "blk", link_pairs(STEPS[link]))
        for p, offset in fresh:
            multiply(p, offset)
            count[offset] = count.get(offset, 0) + 1
        start_batches()
        for i, batch in enumerate(BATCHES[: len(parts)]):
            for name in NEXT:
                if batch.get(name) == number:
                    parts[i] = step(name, parts[i])
        fresh = list(arrived)
        held.update(arrived)
        h_keys, t_keys = list(held), list(terms)
        h, t, parts = lax.optimization_barrier(([held[k] for k in h_keys], [terms[k] for k in t_keys], parts))
        held, terms = dict(zip(h_keys, h)), dict(zip(t_keys, t))
    for p, offset in fresh:
        multiply(p, offset)
        count[offset] = count.get(offset, 0) + 1
    start_batches()
    early, (second, third, last) = jnp.concatenate(parts[:2], axis=1), parts[2:]
    last = step("pack", last)
    third = step("core", third)
    last, third, second, early = lax.optimization_barrier((last, third, second, early))
    last = step("core", last)
    third = sum_z(third)
    last, third, second, early = lax.optimization_barrier((last, third, second, early))
    last = sum_z(last)
    second = step("far", second)
    early = step("y", jnp.concatenate([early, third], axis=1))
    last, second, early = lax.optimization_barrier((last, second, early))
    parts = [early, step("y", jnp.concatenate([second, last], axis=1))]
    order = order[:3] + order[5:7] + order[3:5] + order[7:]

    me = lax.axis_index("blk")
    my_x, my_y = me % NX, me // NX
    everything = jnp.concatenate(parts, axis=1)
    place = [NX * dy + dx for dx, dy in order]
    place_of = jnp.array([place.index(k) for k in range(NX * NY)], jnp.int32)
    columns = []
    for source in range(NX * NY):
        dx = (my_x + NX - source % NX) % NX
        dy = (my_y + NY - source // NX) % NY
        start = place_of[dy * NX + dx] * ij_b
        columns.append(lax.dynamic_slice_in_dim(everything, start, ij_b, axis=1))
    full = jnp.concatenate(columns, axis=1)
    denom = my_energy[:, None] - ij_energy[None, :]
    return jnp.where(my_valid[:, None], full / denom, 0.0).T


def solution(mesh):
    placed = (P("blk", "vslab", None), P("vslab", None, "blk"), P("blk"), P(), P(), P())
    return jax.shard_map(
        on_device, mesh=mesh, in_specs=placed, out_specs=P(None, ("blk", "vslab")), check_vma=False
    )
```

```python
import jax
import jax.numpy as jnp
from jax import lax
from jax.experimental import pallas as pl
from jax.experimental.pallas import tpu as pltpu
from jax.sharding import PartitionSpec as P

NX, NY = 4, 2
STEPS = ((1, 0), (3, 0), (0, 1))
ROUNDS = (
    ((0, 0, (0, 0)), (1, 0, (0, 0)), (2, 0, (0, 0))),
    ((0, 2, (0, 0)), (1, 1, (0, 0)), (2, 2, (0, 0))),
    ((0, 1, (0, 0)), (1, 2, (0, 0)), (2, 1, (3, 0))),
    ((0, 1, (3, 1)), (1, 2, (0, 1)), (2, 0, (3, 0))),
    ((0, 0, (0, 1)), (1, 2, (3, 0)), (2, 1, (1, 0))),
    ((0, 0, (1, 0)), (1, 1, (3, 0)), (2, 2, (1, 0))),
    ((0, 1, (1, 1)), (1, 0, (3, 1)), (2, 2, (2, 0))),
)
BATCHES = (
    {"blocks": 1, "pack": 0, "core": 1, "near": 2, "far": 3},
    {"blocks": 2, "pack": 3, "core": 4, "near": 5, "far": 6},
    {"blocks": 2, "pack": 4, "core": 5, "near": 6},
    {"blocks": 2, "pack": 6},
    {"blocks": 1},
)
NEXT = ("pack", "core", "near", "far", "y")


def moved(offset, step):
    return ((offset[0] + step[0]) % NX, (offset[1] + step[1]) % NY)


def link_pairs(step):
    pairs = []
    for y in range(NY):
        for x in range(NX):
            to_x, to_y = moved((x, y), step)
            pairs.append((y * NX + x, to_y * NX + to_x))
    return pairs


def slot_of_pairs(block_size, block_owner, rows, cap):
    count = block_size.shape[0]
    order = jnp.arange(count, dtype=jnp.int32)
    earlier = order[None, :] < order[:, None]
    starts = jnp.sum(jnp.where(earlier, block_size[None, :], 0), axis=1)
    same = block_owner[:, None] == block_owner[None, :]
    before = jnp.sum(jnp.where(same & earlier, block_size[None, :], 0), axis=1)
    row_ids = jnp.arange(rows, dtype=jnp.int32)
    inside = (row_ids[:, None] >= starts[None, :]) & (
        row_ids[:, None] < (starts + block_size)[None, :]
    )
    base = block_owner * cap + before - starts
    return jnp.sum(jnp.where(inside, base[None, :], 0), axis=1) + row_ids


CHEAP = pl.CostEstimate(flops=1, bytes_accessed=1, transcendentals=0)
PARAMS = pltpu.CompilerParams(vmem_limit_bytes=14 * 2**20)
F32 = jnp.float32


def halves(x):
    high = x.astype(jnp.bfloat16)
    return high, (x - high.astype(F32)).astype(jnp.bfloat16)


def product_kernel(t_ref, v_ref, out_ref):
    t_high, t_low = halves(t_ref[...])
    v_high, v_low = halves(v_ref[...])

    def dot(t, v):
        return lax.dot_general(t, v, (((0,), (0,)), ((), ())), preferred_element_type=F32)

    term = dot(t_high, v_high) + (dot(t_high, v_low) + dot(t_low, v_high))

    @pl.when(pl.program_id(0) == 0)
    def _():
        out_ref[...] = term

    @pl.when(pl.program_id(0) > 0)
    def _():
        out_ref[...] += term


def product(t, v, first):
    depth, rows = t.shape
    steps = 4 if depth % 64 == 0 else 2
    tile, width = depth // steps, v.shape[1]
    return pl.pallas_call(
        product_kernel,
        grid=(steps,),
        in_specs=[
            pl.BlockSpec((tile, rows), lambda k: (k, 0)),
            pl.BlockSpec((pl.Element(tile), pl.Element(width)), lambda k: (pl.multiple_of(first + k * tile, 16), 0)),
        ],
        out_specs=pl.BlockSpec((rows, width), lambda k: (0, 0)),
        out_shape=jax.ShapeDtypeStruct((rows, width), F32),
        cost_estimate=CHEAP,
        compiler_params=PARAMS,
        name="product",
    )(t, v)


def pack_kernel(hot_ref, p_ref, out_ref):
    rest, total = p_ref[...], None
    for _ in range(3):
        part = rest.astype(jnp.bfloat16)
        rest = rest - part.astype(F32)
        term = lax.dot_general(hot_ref[...], part, (((1,), (1,)), ((), ())), preferred_element_type=F32)
        total = term if total is None else total + term
    out_ref[...] = total


def pack(hot, ladder):
    tile = hot.shape[0] // 4
    return pl.pallas_call(
        pack_kernel,
        grid=(4,),
        in_specs=[
            pl.BlockSpec((tile, hot.shape[1]), lambda k: (k, 0)),
            pl.BlockSpec(ladder.shape, lambda k: (0, 0)),
        ],
        out_specs=pl.BlockSpec((tile, ladder.shape[0]), lambda k: (k, 0)),
        out_shape=jax.ShapeDtypeStruct((hot.shape[0], ladder.shape[0]), F32),
        cost_estimate=CHEAP,
        compiler_params=PARAMS,
        name="pack",
    )(hot, ladder)


def on_device(amplitudes, integrals, ab_energy, ij_energy, block_size, block_owner):
    owners = lax.axis_size("vslab")
    ij_b = amplitudes.shape[0]
    rows = integrals.shape[2]
    cap = 3 * rows // owners
    v_matrix = integrals.reshape(-1, rows)
    t_own = amplitudes.transpose(1, 2, 0).reshape(-1, ij_b)
    depth = t_own.shape[0]
    cuts = [0, depth // 96 // 2 * 64, depth - depth // 96 * 32 - 32, depth]

    held = {(p, (0, 0)): t_own[cuts[p] : cuts[p + 1]] for p in range(3)}
    terms = {}

    dest = slot_of_pairs(block_size, block_owner, rows, cap)
    mine = lax.axis_index("vslab")
    slots = jnp.arange(cap, dtype=jnp.int32)
    apart = jnp.array([c + 4 * z + 2 * y for c in (0, 1) for z in (0, 2, 1, 3) for y in (0, 1)], jnp.int32)
    near = mine ^ apart

    def one_hot(owner):
        at = (owner[:, None] * cap + slots[None, :]).reshape(-1)
        return (at[:, None] == dest[None, :]).astype(jnp.bfloat16)

    hot = one_hot(near)
    my_hot = hot[:cap] > 0.5
    my_energy = jnp.sum(jnp.where(my_hot, ab_energy[None, :], 0.0), axis=1)
    my_valid = jnp.any(my_hot, axis=1)

    def multiply(piece, offset):
        term = product(held[piece, offset], v_matrix, cuts[piece])
        terms[offset] = terms[offset] + term if offset in terms else term

    def swap(part, bits):
        return lax.ppermute(part, "vslab", [(i, i ^ bits) for i in range(owners)])

    def fold(part, bits):
        middle = part.shape[0] // 2
        return part[:middle] + swap(part[middle:], bits)

    def sum_z(part):
        width = 2 * cap
        total = part[:width]
        for k, bits in enumerate((8, 4, 12)):
            total = total + swap(part[(k + 1) * width : (k + 2) * width], bits)
        return total

    def step(name, part):
        if name == "pack":
            return pack(hot, part)
        return fold(part, {"core": 1, "near": 4, "far": 8, "y": 2}[name])

    fresh = [(p, (0, 0)) for p in range(3)]
    count = {}
    parts, order = [], []

    def start_batches():
        while len(parts) < len(BATCHES):
            batch = [o for o in terms if count[o] == 3][: BATCHES[len(parts)]["blocks"]]
            if len(batch) < BATCHES[len(parts)]["blocks"]:
                break
            parts.append(jnp.concatenate([terms.pop(o) for o in batch], axis=0))
            order.extend(batch)

    for number, sends in enumerate(ROUNDS):
        arrived = {}
        for link, p, offset in sends:
            to = moved(offset, STEPS[link])
            arrived[p, to] = lax.ppermute(held[p, offset], "blk", link_pairs(STEPS[link]))
        for p, offset in fresh:
            multiply(p, offset)
            count[offset] = count.get(offset, 0) + 1
        start_batches()
        for i, batch in enumerate(BATCHES[: len(parts)]):
            for name in NEXT:
                if batch.get(name) == number:
                    parts[i] = step(name, parts[i])
        fresh = list(arrived)
        held.update(arrived)
        h_keys, t_keys = list(held), list(terms)
        h, t, parts = lax.optimization_barrier(([held[k] for k in h_keys], [terms[k] for k in t_keys], parts))
        held, terms = dict(zip(h_keys, h)), dict(zip(t_keys, t))
    for p, offset in fresh:
        multiply(p, offset)
        count[offset] = count.get(offset, 0) + 1
    start_batches()
    early, (second, third, last) = jnp.concatenate(parts[:2], axis=1), parts[2:]
    last = step("pack", last)
    third = step("core", third)
    last, third, second, early = lax.optimization_barrier((last, third, second, early))
    last = step("core", last)
    third = sum_z(third)
    last, third, second, early = lax.optimization_barrier((last, third, second, early))
    width, split = 2 * cap, second.shape[1]
    away = swap(jnp.concatenate([second[width:], last[width : 2 * width]], axis=1), 8)
    second = second[:width] + away[:, :split]
    last = last[:width] + away[:, split:] + swap(last[2 * width : 3 * width], 4) + swap(last[3 * width :], 12)
    early = step("y", jnp.concatenate([early, third], axis=1))
    last, second, early = lax.optimization_barrier((last, second, early))
    parts = [early, step("y", jnp.concatenate([second, last], axis=1))]
    order = order[:3] + order[5:7] + order[3:5] + order[7:]

    me = lax.axis_index("blk")
    my_x, my_y = me % NX, me // NX
    everything = jnp.concatenate(parts, axis=1)
    place = [NX * dy + dx for dx, dy in order]
    place_of = jnp.array([place.index(k) for k in range(NX * NY)], jnp.int32)
    columns = []
    for source in range(NX * NY):
        dx = (my_x + NX - source % NX) % NX
        dy = (my_y + NY - source // NX) % NY
        start = place_of[dy * NX + dx] * ij_b
        columns.append(lax.dynamic_slice_in_dim(everything, start, ij_b, axis=1))
    full = jnp.concatenate(columns, axis=1)
    denom = my_energy[:, None] - ij_energy[None, :]
    return jnp.where(my_valid[:, None], full / denom, 0.0).T


def solution(mesh):
    placed = (P("blk", "vslab", None), P("vslab", None, "blk"), P("blk"), P(), P(), P())
    return jax.shard_map(
        on_device, mesh=mesh, in_specs=placed, out_specs=P(None, ("blk", "vslab")), check_vma=False
    )
```
